32 devices in a mesh: req: 2 (over core), seq: 16 (over z, y, x).
Axes of the slice: x: 2, y: 2, z: 4, core: 2. Of those that a mesh axis runs over, the one named last changes fastest.
Arguments:
- tokens: bfloat16 [4, 32, 1536], P(None, ('req', 'seq')), may hold values from -6 to 6
- lengths: int32 [32], P('req'), may hold values from 1 to 16384, as said below
- k_cache: bfloat16 [32, 4096, 256], P('req', 'seq'), may hold values from -500 to 500
- v_cache: bfloat16 [32, 4096, 256], P('req', 'seq'), may hold values from -12 to 12
- attn_gain: bfloat16 [1536], replicated, may hold values from 0.5 to 1.5
- w_qkv: bfloat16 [1536, 2048], replicated, may hold values from -0.15625 to 0.15625
- sink: float32 [12], replicated, may hold values from -1 to 3
- w_out: bfloat16 [1536, 1536], replicated, may hold values from -0.15625 to 0.15625
- moe_gain: bfloat16 [1536], replicated, may hold values from 0.5 to 1.5
- router: bfloat16 [1536, 32], replicated, may hold values from -0.15625 to 0.15625
- w_gate: bfloat16 [1536, 24576], P(None, ('req', 'seq')), may hold values from -0.15625 to 0.15625
- w_up: bfloat16 [1536, 24576], P(None, ('req', 'seq')), may hold values from -0.15625 to 0.15625
- w_down: bfloat16 [24576, 1536], P(('req', 'seq')), may hold values from -0.21875 to 0.21875
- routes: int32 [32, 4, 4], replicated, may hold values from 0 to 31, all different within a row; in each aligned block of 4 rows (0 to 3, 4 to 7, ..., all dimensions but the last counted through in order) at most 2 rows name the same one
Outputs:
- outputs: bfloat16 [4, 32, 1536], P(None, ('req', 'seq'))
The draws below stay inside these ranges and needn't reach their ends.
Inputs may be any that keep to these rules, and one draw needn't show every extreme that they name: Each request has lengths positions before the first step; some request has all 16384 in every draw. `routes`: among the 4 tokens of one device's requests (requests 1 d .. 1 d + 1 - 1, all steps), no expert is named by more than 2 tokens, and in every draw some expert is named by exactly 2.
All inputs are finite; a program needn't handle non-finite values.
Results may differ from the reference program's by a relative error of at most 0.02.
Values may be sent and summed in bfloat16 or wider, within the bound.
A program may use at most 512 MiB of HBM per device.

```python
import math
import jax
import jax.numpy as jnp
import numpy as np
from jax import lax

D = 1536
QH = 12
KVH = 2
HD = 128
E = 32
EFF = 768
TOP = 4
STEPS = 4
MOST = 2
ROWS_DEV = 1
CACHE = 4096
SPAN = 16384
B = 32
WINDOW = 4096


def draw_lengths(key, part):
    first, second, third = jax.random.split(jax.random.fold_in(key, 11), 3)
    left = jax.random.randint(first, (B,), 0, SPAN)
    right = jax.random.randint(second, (B,), 0, SPAN)
    spans = 1 + left * right // SPAN
    filled = jax.random.randint(third, (4,), 0, B)
    return spans.at[filled].set(SPAN).astype(jnp.int32)


def draw_k_cache(key, part):
    first = jax.random.fold_in(jax.random.fold_in(key, 23), 0)
    values = jnp.clip(2.0 * jax.random.normal(first, (B, CACHE, KVH * HD), jnp.float32), -12.0, 12.0)
    return values.astype(jnp.bfloat16)


def steps_of(rng, shape, cuts, low, top_value):
    level, own = 1.0, jax.random.fold_in(rng, 6)
    for dim, parts in cuts:
        draws = jnp.exp(jax.random.uniform(jax.random.fold_in(own, dim), (parts,), jnp.float32, low / len(cuts), top_value / len(cuts)))
        level = level * jnp.repeat(draws, shape[dim] // parts).reshape([-1 if axis == dim else 1 for axis in range(len(shape))])
    return level


def assign_block(stream_key, own, number, rows, count, top, bound, skew):
    order = jax.random.permutation(stream_key, count)
    packed, usual = portions_of(count, rows * top, bound, skew, True), portions_of(count, rows * top, bound, skew, False)
    places = jnp.arange(count)

    def named(sizes, turn):
        used = int((sizes > 0).sum())
        fixed = max(1, used // 4)
        passed = fixed + (places - fixed + turn * (used - fixed)) % max(1, count - fixed)
        return jnp.zeros((count,), jnp.int32).at[order[jnp.where(places < fixed, places, passed)]].set(jnp.asarray(sizes, jnp.int32))

    sizes = jnp.where(number % 4 == 0, named(packed, number // 4), named(usual, number - number // 4 - 1))
    mixed = jax.random.permutation(jax.random.fold_in(own, 3), count)
    source_of, taker = mixed[0:count // 2 * 2:2], mixed[1:count // 2 * 2:2]
    room = jnp.minimum(sizes[source_of] - 1, bound - sizes[taker]) // 2
    room = jnp.where((source_of == order[0]) | (taker == order[0]) | (sizes[taker] == 0), 0, jnp.maximum(room, 0))
    passed = jax.random.randint(jax.random.fold_in(own, 4), (count // 2,), 0, 1 << 20) % (room + 1)
    sizes = sizes.at[source_of].add(-passed).at[taker].add(passed)
    labels = jnp.searchsorted(jnp.cumsum(sizes), jnp.arange(rows * top), side="right").astype(jnp.int32)
    table = labels.reshape(top, rows).T
    table = table[jax.random.permutation(jax.random.fold_in(own, 1), rows)]
    turn = jax.random.randint(jax.random.fold_in(own, 2), (rows, 1), 0, top)
    return jnp.take_along_axis(table, (jnp.arange(top)[None, :] + turn) % top, axis=1)


def portions_of(count, total, reach, lean, full):
    loads = [(1 << 20) // math.isqrt(grade ** lean) + 1 for grade in range(1, count + 1)]
    largest = reach if full else min(reach, max(-(-total // count), total * loads[0] // sum(loads)))
    least = 1 if total - largest >= count - 1 else 0
    given, surplus = [largest] + [least] * (count - 1), total - largest - least * (count - 1)
    while surplus > 0:
        movable = [i for i in range(1, count) if given[i] < largest] or [i for i in range(1, count) if given[i] < reach]
        whole, left = sum([loads[i] for i in movable]), surplus
        for i in movable:
            more = min(reach - given[i], max(1, left * loads[i] // whole), surplus)
            given[i] = given[i] + more
            surplus = surplus - more
    return np.array(given)


def scatter_about(stream_key, extent, deviation, reach, cuts=(), kind=jnp.bfloat16):
    drawn = deviation * jax.random.normal(stream_key, extent, jnp.float32)
    if cuts:
        drawn = drawn * steps_of(stream_key, extent, cuts, -0.22, 0.18)
    return jnp.clip(drawn, -reach, reach).astype(kind)


def setup_inputs(seed: int = 0) -> dict:
    key_of = jax.random.split(jax.random.key(seed), 15)
    tokens = scatter_about(key_of[0], (STEPS, B, D), 1.0, 6.0, ((1, 32),))
    lengths = draw_lengths(jax.random.fold_in(key_of[14], 71), 0)
    k_cache = draw_k_cache(jax.random.fold_in(key_of[14], 71), 0)
    v_cache = scatter_about(key_of[3], (B, CACHE, KVH * HD), 2.0, 12.0, ((0, 2), (1, 16)))
    attn_gain = jnp.clip(1.0 + 0.1 * jax.random.normal(key_of[4], (D,), jnp.float32), 0.5, 1.5).astype(jnp.bfloat16)
    w_qkv = scatter_about(key_of[5], (D, (QH + 2 * KVH) * HD), D ** -0.5, 0.15625)
    sink = jnp.clip(jax.random.uniform(key_of[6], (QH,), jnp.float32, -1.0, 3.0), -1.0, 3.0)
    w_out = scatter_about(key_of[7], (QH * HD, D), (QH * HD) ** -0.5, 0.15625)
    moe_gain = jnp.clip(1.0 + 0.1 * jax.random.normal(key_of[8], (D,), jnp.float32), 0.5, 1.5).astype(jnp.bfloat16)
    router = scatter_about(key_of[9], (D, E), D ** -0.5, 0.15625)
    w_gate = scatter_about(key_of[10], (D, E * EFF), D ** -0.5, 0.15625, ((1, 32),))
    w_up = scatter_about(key_of[11], (D, E * EFF), D ** -0.5, 0.15625, ((1, 32),))
    w_down = scatter_about(key_of[12], (E * EFF, D), EFF ** -0.5, 0.21875, ((0, 32),))
    routes_keys = jax.random.split(jax.random.fold_in(key_of[13], 1), B * STEPS // (ROWS_DEV * STEPS))
    routes_turns = jax.random.permutation(jax.random.fold_in(key_of[13], 3), B * STEPS // (ROWS_DEV * STEPS))
    routes = jax.vmap(lambda own, number: assign_block(jax.random.fold_in(key_of[13], 2), own, number, ROWS_DEV * STEPS, E, TOP, MOST, 2))(routes_keys, routes_turns).reshape((B, STEPS, TOP))
    return dict(tokens=tokens, lengths=lengths, k_cache=k_cache, v_cache=v_cache, attn_gain=attn_gain, w_qkv=w_qkv, sink=sink, w_out=w_out, moe_gain=moe_gain, router=router, w_gate=w_gate, w_up=w_up, w_down=w_down, routes=routes)


def normalize(x, gain):
    xf = x.astype(jnp.float32)
    inv = lax.rsqrt(lax.optimization_barrier(jnp.mean(xf * xf, axis=-1, keepdims=True)) + 1e-05)
    return (xf * inv * gain.astype(jnp.float32)).astype(jnp.bfloat16)

def rotate(x, place):
    half = x.shape[-1] // 2
    index = jnp.arange(half, dtype=jnp.float32)
    inverse = jnp.exp(-jnp.log(1000000.0) * 2.0 * index / x.shape[-1])
    angle = place.astype(jnp.float32)[..., None, None] * inverse
    first = x[..., :half]
    second = x[..., half:]
    cosine = jnp.cos(angle)
    sine = jnp.sin(angle)
    return jnp.concatenate([first * cosine - second * sine, second * cosine + first * sine], axis=-1)

def reference(tokens, lengths, k_cache, v_cache, attn_gain, w_qkv, sink, w_out, moe_gain, router, w_gate, w_up, w_down, routes):
    heads_per = QH // KVH
    scale = HD ** (-0.5)
    block = 16
    tail_keys = jnp.zeros((B, STEPS, KVH, HD), jnp.bfloat16)
    tail_vals = jnp.zeros((B, STEPS, KVH, HD), jnp.bfloat16)
    gate_e = w_gate.reshape(D, E, EFF).transpose(1, 0, 2)
    up_e = w_up.reshape(D, E, EFF).transpose(1, 0, 2)
    down_e = w_down.reshape(E, EFF, D)
    sink_grid = sink.astype(jnp.float32).reshape(KVH, heads_per)
    results = []
    for step in range(STEPS):
        x = tokens[step]
        a = normalize(x, attn_gain)
        proj = jnp.dot(a, w_qkv, preferred_element_type=jnp.float32)
        place = lengths + step
        query = rotate(proj[:, :QH * HD].reshape(B, QH, HD), place).astype(jnp.bfloat16)
        fresh_key = rotate(proj[:, QH * HD:(QH + KVH) * HD].reshape(B, KVH, HD), place).astype(jnp.bfloat16)
        fresh_val = proj[:, (QH + KVH) * HD:].reshape(B, KVH, HD).astype(jnp.bfloat16)
        tail_keys = tail_keys.at[:, step].set(fresh_key)
        tail_vals = tail_vals.at[:, step].set(fresh_val)

        def attend(pieces):
            qb, kc, vc, lb, tk, tv = pieces
            count = qb.shape[0]
            qg = qb.astype(jnp.float32).reshape(count, KVH, heads_per, HD)
            kf = kc.astype(jnp.float32).reshape(count, CACHE, KVH, HD)
            vf = vc.astype(jnp.float32).reshape(count, CACHE, KVH, HD)
            scores = jnp.einsum('nkgd,nckd->nkgc', qg, kf) * scale
            key_slot = jnp.arange(CACHE, dtype=jnp.int32)
            back = jnp.mod(lb[:, None] - 1 - key_slot[None, :], WINDOW)
            valid = back < jnp.minimum(lb, WINDOW - 1 - step)[:, None]
            valid = valid[:, None, None, :]
            tail_scores = jnp.einsum('nkgd,nskd->nkgs', qg, tk.astype(jnp.float32)) * scale
            tail_valid = (jnp.arange(STEPS) <= step)[None, None, None, :]
            top = jnp.maximum(lax.optimization_barrier(jnp.max(jnp.where(valid, scores, -1e+30), axis=-1)), lax.optimization_barrier(jnp.max(jnp.where(tail_valid, tail_scores, -1e+30), axis=-1)))
            top = jnp.maximum(top, sink_grid[None])
            weights = jnp.where(valid, jnp.exp(scores - top[..., None]), 0.0)
            tail_w = jnp.where(tail_valid, jnp.exp(tail_scores - top[..., None]), 0.0)
            total = lax.optimization_barrier(jnp.sum(weights, axis=-1)) + lax.optimization_barrier(jnp.sum(tail_w, axis=-1)) + jnp.exp(sink_grid[None] - top)
            rounded = lax.optimization_barrier(weights.astype(jnp.bfloat16)).astype(jnp.float32)
            tail_rounded = lax.optimization_barrier(tail_w.astype(jnp.bfloat16)).astype(jnp.float32)
            mixed = jnp.einsum('nkgc,nckd->nkgd', rounded, vf) + jnp.einsum('nkgs,nskd->nkgd', tail_rounded, tv.astype(jnp.float32))
            return (mixed / total[..., None]).reshape(count, QH * HD).astype(jnp.bfloat16)
        shaped = (query.reshape(B // block, block, QH, HD), k_cache.reshape(B // block, block, CACHE, KVH * HD), v_cache.reshape(B // block, block, CACHE, KVH * HD), lengths.reshape(B // block, block), tail_keys.reshape(B // block, block, STEPS, KVH, HD), tail_vals.reshape(B // block, block, STEPS, KVH, HD))
        attn = lax.map(attend, shaped).reshape(B, QH * HD)
        h = (x.astype(jnp.float32) + jnp.dot(attn, w_out, preferred_element_type=jnp.float32)).astype(jnp.bfloat16)
        u = normalize(h, moe_gain)
        logits = jnp.dot(u, router, preferred_element_type=jnp.float32)
        picks = routes[:, step]
        chosen = jnp.take_along_axis(logits, picks, axis=1)
        share = jax.nn.softmax(chosen, axis=-1)
        dense = lax.optimization_barrier(jnp.sum(share[:, :, None] * (picks[:, :, None] == jnp.arange(E, dtype=jnp.int32)[None, None, :]).astype(jnp.float32), axis=1))

        def expert_step(total, pieces):
            gate_w, up_w, down_w, column = pieces
            hidden = (jax.nn.relu(jnp.dot(u, gate_w, preferred_element_type=jnp.float32)) * jnp.dot(u, up_w, preferred_element_type=jnp.float32)).astype(jnp.bfloat16)
            return (total + column[:, None] * jnp.dot(hidden, down_w, preferred_element_type=jnp.float32), None)
        moe, unused = lax.scan(expert_step, jnp.zeros((B, D), jnp.float32), (gate_e, up_e, down_e, dense.T))
        results.append((h.astype(jnp.float32) + moe).astype(jnp.bfloat16))
    return jnp.stack(results, axis=0)
```

```python
import functools

import jax
import jax.numpy as jnp
from jax import lax
from jax.experimental import pallas as pl
from jax.experimental.pallas import tpu as pltpu
from jax.sharding import PartitionSpec as P

D = 1536
QH = 12
KVH = 2
HD = 128
E = 32
EFF = 768
TOP = 4
STEPS = 4
MOST = 2

ROWS = QH * STEPS
HALF = ROWS // KVH
MSG = ROWS + 16
UG = 4
UL = D // UG
OG = 6
OL = D // OG
BLK = 32
MESH = pl.DeviceIdType.MESH
F32 = jnp.float32
BF16 = jnp.bfloat16


def iota(shape, axis):
    return lax.broadcasted_iota(jnp.int32, shape, axis)


def normed(xf, gain):
    inv = lax.rsqrt(jnp.mean(xf * xf, axis=-1, keepdims=True) + 1e-05)
    return xf * inv * gain


def split3(v):
    hi = v.astype(BF16).astype(F32)
    mid = (v - hi).astype(BF16).astype(F32)
    return hi, mid, v - hi - mid


def kernel(
    nr, ns, blk, lens, x_ref, again_ref, mgain_ref, rope_ref, sink_ref, rall_ref, rown_ref, router_ref,
    kc_hbm, vc_hbm, wqkv_hbm, wout_hbm, wg_hbm, wu_hbm, wd_hbm,
    out_ref,
    wqkv, wout, wg, wu, wd, kc, vc,
    qf, kf, vf, q_all, part, part_in, uf, rows_all, prod_out, prod_in, coef,
    wsem, q_s, q_r, p_s, p_r, u_s, u_r, f_s, o_s, o_r,
):
    devs = nr * ns
    req = lax.axis_index("req")
    seq = lax.axis_index("seq")
    me = req * ns + seq
    lpos = kc.shape[1]
    window = lpos * ns
    cols = wg.shape[1]
    scale = HD ** (-0.5)
    per = EFF // cols
    shift = per.bit_length() - 1

    qparts = 4
    qrows = D // qparts
    loads = [
        pltpu.make_async_copy(
            wqkv_hbm.at[pl.ds(i * qrows, qrows)], wqkv.at[pl.ds(i * qrows, qrows)], wsem.at[i]
        )
        for i in range(qparts)
    ]
    rest = [
        pltpu.make_async_copy(src, dst, wsem.at[qparts + i])
        for i, (src, dst) in enumerate(
            [(kc_hbm, kc), (vc_hbm, vc), (wout_hbm, wout), (wg_hbm, wg), (wu_hbm, wu), (wd_hbm, wd)]
        )
    ]
    for c in loads + rest:
        c.start()
    load_k, load_v, load_out, load_g, load_u, load_d = rest

    barrier = pltpu.get_barrier_semaphore()

    def greet(i, carry):
        d = lax.rem(me + i, devs)
        pl.semaphore_signal(
            barrier, inc=1, device_id=(d // ns, lax.rem(d, ns)), device_id_type=MESH
        )
        return carry

    lax.fori_loop(1, devs, greet, 0)

    xf = x_ref[...].astype(F32)
    a = normed(xf, again_ref[...].astype(F32)).astype(BF16)
    proj = jnp.zeros((STEPS, wqkv.shape[1]), F32)
    for i in range(qparts):
        loads[i].wait()
        proj = proj + jnp.dot(
            a[:, i * qrows : (i + 1) * qrows],
            wqkv[i * qrows : (i + 1) * qrows, :],
            preferred_element_type=F32,
        )
    cosine = rope_ref[0:STEPS, :]
    sine = rope_ref[STEPS : 2 * STEPS, :]

    def rotated(head):
        v = proj[:, head * HD : (head + 1) * HD]
        return v * cosine + pltpu.roll(v, HD // 2, 1) * sine

    for head in range(QH):
        qf[head * STEPS : (head + 1) * STEPS, :] = rotated(head)
    kf[...] = jnp.zeros_like(kf)
    vf[...] = jnp.zeros_like(vf)
    for head in range(KVH):
        kf[head * STEPS : (head + 1) * STEPS, :] = rotated(QH + head)
        vf[head * STEPS : (head + 1) * STEPS, :] = proj[
            :, (QH + KVH + head) * HD : (QH + KVH + head + 1) * HD
        ]
    own_q = qf[...].astype(BF16)
    q_all[seq] = own_q

    pl.semaphore_wait(barrier, devs - 1)

    def q_copy(peer, slot, k):
        return pltpu.make_async_remote_copy(
            src_ref=q_all.at[seq], dst_ref=q_all.at[slot], send_sem=q_s.at[k],
            recv_sem=q_r.at[slot], device_id=(req, peer), device_id_type=MESH,
        )

    def q_send(i, carry):
        peer = lax.rem(seq + i, ns)
        q_copy(peer, seq, peer).start()
        return carry

    lax.fori_loop(1, ns, q_send, 0)

    row = iota((ROWS, HD), 0)
    lane = iota((ROWS, HD), 1)
    eye = row == lane

    def to_row(col):
        return jnp.sum(jnp.where(eye, col, 0.0), axis=0, keepdims=True)

    def to_col(r):
        return jnp.sum(jnp.where(eye, r, 0.0), axis=1, keepdims=True)

    tail = (
        lax.dot_general(
            own_q, kf[...].astype(BF16), (((1,), (1,)), ((), ())), preferred_element_type=F32
        )
        * scale
    )
    upper = (row >= HALF).astype(jnp.int32)
    fresh = ((lane >> 2) == upper) & ((lane & 3) <= (row & 3))
    tail = jnp.where(fresh, tail, jnp.where(lane == KVH * STEPS, sink_ref[...], -1e30))
    tail_peak = jnp.max(tail, axis=1, keepdims=True)
    tail_w = jnp.exp(tail - tail_peak)
    tail_total = jnp.sum(tail_w, axis=1, keepdims=True)
    tail_mixed = jnp.dot(
        tail_w.astype(BF16), vf[...].astype(BF16), preferred_element_type=F32
    )

    load_k.wait()
    load_v.wait()

    first = jnp.where(row < HALF, 1.0, 0.0).astype(BF16)
    second = jnp.where(row < HALF, 0.0, 1.0).astype(BF16)
    slot_id = seq * lpos + iota((ROWS, lpos), 1)
    step_id = iota((ROWS, lpos), 0) & 3
    stat_row = iota((16, HD), 0)

    def q_wait(i, carry):
        peer = lax.rem(seq + i, ns)
        q_copy(peer, peer, peer).wait_recv()
        return carry

    lax.fori_loop(1, ns, q_wait, 0)

    def p_copy(peer, slot, k):
        return pltpu.make_async_remote_copy(
            src_ref=part.at[peer], dst_ref=part_in.at[slot], send_sem=p_s.at[k],
            recv_sem=p_r.at[slot], device_id=(req, peer), device_id_type=MESH,
        )

    def attend(n):
        q = q_all[n]
        wide = jnp.concatenate([q * first, q * second], axis=1)
        s = (
            lax.dot_general(wide, kc[n], (((1,), (1,)), ((), ())), preferred_element_type=F32)
            * scale
        )
        length = lens[n]
        back = (length - 1 - slot_id) & (window - 1)
        valid = back < jnp.minimum(length, window - 1 - step_id)
        peak = jnp.max(jnp.where(valid, s, -1e30), axis=1, keepdims=True)
        w = jnp.where(valid, jnp.exp(s - peak), 0.0)
        total = jnp.sum(w, axis=1, keepdims=True)
        both = jnp.dot(w.astype(BF16), vc[n], preferred_element_type=F32)
        mixed = jnp.where(row < HALF, both[:, :HD], both[:, HD:])
        stats = jnp.zeros((16, HD), F32)
        for k, v in enumerate(split3(to_row(peak)) + split3(to_row(total))):
            stats = jnp.where(stat_row == k, v, stats)
        return mixed.astype(BF16), stats.astype(BF16)

    group = 4

    def attend_some(b, carry):
        for j in range(group):
            n = lax.rem(seq + 1 + b * group + j, ns)
            mixed, stats = attend(n)
            part[n, 0:ROWS, :] = mixed
            part[n, ROWS:MSG, :] = stats
        for j in range(group):
            i = b * group + j
            n = lax.rem(seq + 1 + i, ns)

            @pl.when(i < ns - 1)
            def _():
                p_copy(n, seq, n).start()

        return carry

    lax.fori_loop(0, ns // group, attend_some, 0)
    part_in[seq] = part[seq]

    def p_wait(i, carry):
        peer = lax.rem(seq + i, ns)
        p_copy(peer, peer, peer).wait_recv()
        return carry

    lax.fori_loop(1, ns, p_wait, 0)

    peaks, totals = [], []
    for j in range(ns):
        st = part_in[j, ROWS:MSG, :].astype(F32)
        peaks.append(st[0:1] + st[1:2] + st[2:3])
        totals.append(st[3:4] + st[4:5] + st[5:6])
    top = to_row(tail_peak)
    for p in peaks:
        top = jnp.maximum(top, p)
    total_row = jnp.zeros((1, HD), F32)
    mixed = jnp.zeros((ROWS, HD), F32)
    for j in range(ns):
        share = jnp.exp(peaks[j] - top)
        total_row = total_row + share * totals[j]
        mixed = mixed + to_col(share) * part_in[j, 0:ROWS, :].astype(F32)
    tail_share = jnp.exp(tail_peak - to_col(top))
    denom = to_col(total_row) + tail_total * tail_share
    qf[...] = (mixed + tail_mixed * tail_share) / denom
    attn = jnp.concatenate(
        [qf[head * STEPS : (head + 1) * STEPS, :] for head in range(QH)], axis=1
    ).astype(BF16)
    load_out.wait()
    h = (xf + jnp.dot(attn, wout[...], preferred_element_type=F32)).astype(BF16).astype(F32)
    u = normed(h, mgain_ref[...].astype(F32)).astype(BF16)
    u32 = u.astype(F32)
    for g in range(UG):
        uf[g * STEPS : (g + 1) * STEPS, :] = u32[:, g * UL : (g + 1) * UL]
    rows_all[me] = uf[...].astype(BF16)

    def u_copy(slot, k, peer):
        return pltpu.make_async_remote_copy(
            src_ref=rows_all.at[slot], dst_ref=rows_all.at[slot], send_sem=u_s.at[k],
            recv_sem=u_r.at[slot], device_id=(req, peer), device_id_type=MESH,
        )

    def f_copy(slot, k):
        return pltpu.make_async_remote_copy(
            src_ref=rows_all.at[slot], dst_ref=rows_all.at[slot], send_sem=f_s.at[k],
            recv_sem=u_r.at[slot], device_id=(1 - req, seq), device_id_type=MESH,
        )

    def u_send(i, carry):
        peer = lax.rem(seq + i, ns)
        u_copy(me, peer, peer).start()
        return carry

    lax.fori_loop(1, ns, u_send, 0)
    f_copy(me, seq).start()

    rown = rown_ref[...]
    logits = jnp.dot(u, router_ref[...], preferred_element_type=F32)
    expert = iota((STEPS, E), 1)
    chosen = [
        jnp.sum(jnp.where(rown[:, k : k + 1] == expert, logits, 0.0), axis=1, keepdims=True)
        for k in range(TOP)
    ]
    peak = functools.reduce(jnp.maximum, chosen)
    raised = [jnp.exp(c - peak) for c in chosen]
    norm = functools.reduce(jnp.add, raised)
    shares = [r / norm for r in raised]

    width = blk * 16
    nblk = devs // blk
    lane4 = iota((STEPS, width), 1)
    step4 = iota((STEPS, width), 0)
    coefs = []
    for b in range(nblk):
        source = ((lane4 >> 4) + b * blk) >> shift
        hit = jnp.zeros((STEPS, width), F32)
        dense = jnp.zeros((STEPS, width), F32)
        for k in range(TOP):
            same = rown[:, k : k + 1] == source
            hit = jnp.where(same, 1.0, hit)
            dense = jnp.where(same, shares[k], dense)
        slot = jnp.zeros((STEPS, width), F32)
        for t in range(STEPS - 1):
            slot = slot + jnp.where(step4 > t, hit[t : t + 1], 0.0)
        mine = (hit > 0.0) & (slot == (lane4 & 1).astype(F32))
        dense = jnp.where(mine, dense, 0.0)
        for k, v in enumerate(split3(dense)):
            for g in range(OG):
                at = (k * OG + g) * STEPS
                coef[b, at : at + STEPS, :] = jnp.where(((lane4 & 15) >> 1) == g, v, 0.0)

    expert_mine = (me * cols) // EFF
    pick_rows = UG * blk * MOST
    prow = iota((pick_rows, width), 0)
    plane = iota((pick_rows, width), 1)
    piece = prow // (blk * MOST)
    source_row = prow & (blk * MOST - 1)
    place_ok = ((plane >> 4) == (source_row >> 1)) & (((plane & 15) >> 2) == piece)
    want = (source_row & 1).astype(F32)
    lane8 = iota((8, width), 1)
    picks = []
    for b in range(nblk):
        hit = jnp.zeros((8, width), F32)
        for k in range(TOP):
            named = jnp.broadcast_to(rall_ref[k : k + 1, b * width : (b + 1) * width], (8, width))
            hit = jnp.where(named == expert_mine, 1.0, hit)
        slot = jnp.zeros((8, width), F32)
        for t in range(1, STEPS):
            slot = slot + jnp.where((lane8 & 3) >= t, pltpu.roll(hit, t, 1), 0.0)
        code = jnp.where(hit > 0.0, slot, -1.0)[0:1]
        picks.append(jnp.where(place_ok & (code == want), 1.0, 0.0).astype(BF16))

    out_rows = iota((width, OG * blk * MOST), 0)
    out_lane = iota((width, OG * blk * MOST), 1)
    out_piece = out_lane // (blk * MOST)
    out_source = out_lane & (blk * MOST - 1)
    spread = jnp.where(
        ((out_rows >> 4) == (out_source >> 1))
        & ((out_rows & 15) == out_piece * MOST + (out_source & 1)),
        1.0,
        0.0,
    ).astype(BF16)

    def u_wait(i, carry):
        peer = lax.rem(seq + i, ns)
        u_copy(req * ns + peer, peer, peer).wait_recv()
        f_copy(req * ns + peer, peer).start()
        return carry

    lax.fori_loop(1, ns, u_wait, 0)

    def f_wait(i, carry):
        peer = lax.rem(seq + i, ns)
        f_copy((1 - req) * ns + peer, peer).wait_recv()
        return carry

    lax.fori_loop(0, ns, f_wait, 0)

    taken = []
    for b in range(nblk):
        got = jnp.dot(
            picks[b],
            rows_all[b * blk : (b + 1) * blk].reshape(width, UL),
            preferred_element_type=F32,
        ).astype(BF16)
        taken.append(
            jnp.concatenate(
                [got[g * blk * MOST : (g + 1) * blk * MOST] for g in range(UG)], axis=1
            )
        )
    taken = jnp.concatenate(taken, axis=0) if nblk > 1 else taken[0]
    load_g.wait()
    load_u.wait()
    load_d.wait()
    gate = jnp.dot(taken, wg[...], preferred_element_type=F32)
    hidden = jnp.maximum(gate, 0.0) * jnp.dot(taken, wu[...], preferred_element_type=F32)
    made = jnp.dot(hidden.astype(BF16), wd[...], preferred_element_type=F32).astype(BF16)
    for b in range(nblk):
        stacked = jnp.concatenate(
            [
                made[b * blk * MOST : (b + 1) * blk * MOST, g * OL : (g + 1) * OL]
                for g in range(OG)
            ],
            axis=0,
        )
        prod_out[b * blk : (b + 1) * blk] = (
            jnp.dot(spread, stacked, preferred_element_type=F32).astype(BF16).reshape(blk, 16, OL)
        )

    def o_copy(d, slot, k):
        return pltpu.make_async_remote_copy(
            src_ref=prod_out.at[d], dst_ref=prod_in.at[slot], send_sem=o_s.at[k],
            recv_sem=o_r.at[slot], device_id=(d // ns, lax.rem(d, ns)), device_id_type=MESH,
        )

    def o_send(i, carry):
        d = lax.rem(me + i, devs)
        o_copy(d, me, d).start()
        return carry

    lax.fori_loop(1, devs, o_send, 0)
    prod_in[me] = prod_out[me]

    def o_wait(i, carry):
        d = lax.rem(me + i, devs)
        o_copy(d, d, d).wait_recv()
        return carry

    lax.fori_loop(1, devs, o_wait, 0)

    moe = jnp.zeros((3 * OG * STEPS, OL), F32)
    for b in range(nblk):
        moe = moe + jnp.dot(
            coef[b].astype(BF16),
            prod_in[b * blk : (b + 1) * blk].reshape(width, OL),
            preferred_element_type=F32,
        )
    span = OG * STEPS
    moe = moe[0:span] + moe[span : 2 * span] + moe[2 * span : 3 * span]
    moe = jnp.concatenate([moe[g * STEPS : (g + 1) * STEPS] for g in range(OG)], axis=1)
    out_ref[...] = (h + moe).astype(BF16)

    def drain(i, carry):
        peer = lax.rem(seq + i, ns)
        q_copy(peer, seq, peer).wait_send()
        p_copy(peer, seq, peer).wait_send()
        u_copy(me, peer, peer).wait_send()
        f_copy(req * ns + peer, peer).wait_send()
        return carry

    lax.fori_loop(1, ns, drain, 0)
    f_copy(me, seq).wait_send()

    def o_drain(i, carry):
        d = lax.rem(me + i, devs)
        o_copy(d, me, d).wait_send()
        return carry

    lax.fori_loop(1, devs, o_drain, 0)


def on_device(
    nr, ns, tokens, lengths, k_cache, v_cache, attn_gain, w_qkv, sink, w_out, moe_gain, router,
    w_gate, w_up, w_down, routes,
):
    seq = lax.axis_index("seq")
    device = lax.axis_index("req") * ns + seq
    devs = nr * ns
    blk = min(BLK, devs)
    lpos = k_cache.shape[1]
    group = lengths.shape[0]
    cols = w_gate.shape[1]
    half = HD // 2
    own_len = lax.dynamic_slice_in_dim(lengths, seq, 1)
    place = own_len + jnp.arange(STEPS, dtype=jnp.int32)
    inverse = jnp.exp(-jnp.log(1000000.0) * 2.0 * jnp.arange(half, dtype=F32) / HD)
    angle = place.astype(F32)[:, None] * inverse
    cosine, sine = jnp.cos(angle), jnp.sin(angle)
    rope = jnp.concatenate(
        [jnp.concatenate([cosine, cosine], 1), jnp.concatenate([-sine, sine], 1)], 0
    )
    sinks = jnp.broadcast_to(jnp.repeat(sink, STEPS)[:, None], (ROWS, HD))
    rall = jnp.broadcast_to(
        routes.transpose(2, 0, 1)[:, :, None, :], (TOP, devs, 4, STEPS)
    ).reshape(TOP, devs * 16)
    rown = lax.dynamic_index_in_dim(routes, device, 0, False)

    vmem = pl.BlockSpec(memory_space=pltpu.VMEM)
    smem = pl.BlockSpec(memory_space=pltpu.SMEM)
    hbm = pl.BlockSpec(memory_space=pl.ANY)
    dma = pltpu.SemaphoreType.DMA
    out = pl.pallas_call(
        functools.partial(kernel, nr, ns, blk),
        out_shape=jax.ShapeDtypeStruct((STEPS, D), BF16),
        in_specs=[smem] + [vmem] * 8 + [hbm] * 7,
        out_specs=vmem,
        scratch_shapes=[
            pltpu.VMEM(w_qkv.shape, BF16),
            pltpu.VMEM(w_out.shape, BF16),
            pltpu.VMEM(w_gate.shape, BF16),
            pltpu.VMEM(w_up.shape, BF16),
            pltpu.VMEM(w_down.shape, BF16),
            pltpu.VMEM((group, lpos, KVH * HD), BF16),
            pltpu.VMEM((group, lpos, KVH * HD), BF16),
            pltpu.VMEM((ROWS, HD), F32),
            pltpu.VMEM((HD, HD), F32),
            pltpu.VMEM((HD, HD), F32),
            pltpu.VMEM((ns, ROWS, HD), BF16),
            pltpu.VMEM((ns, MSG, HD), BF16),
            pltpu.VMEM((ns, MSG, HD), BF16),
            pltpu.VMEM((UG * STEPS, UL), F32),
            pltpu.VMEM((devs, UG * STEPS, UL), BF16),
            pltpu.VMEM((devs, 16, OL), BF16),
            pltpu.VMEM((devs, 16, OL), BF16),
            pltpu.VMEM((devs // blk, 3 * OG * STEPS, blk * 16), F32),
            dma((10,)), dma((ns,)), dma((ns,)), dma((ns,)), dma((ns,)), dma((ns,)),
            dma((devs,)), dma((ns,)), dma((devs,)), dma((devs,)),
        ],
        compiler_params=pltpu.CompilerParams(
            collective_id=0, has_side_effects=True, vmem_limit_bytes=56 * 1024 * 1024
        ),
    )(
        lengths, tokens.reshape(STEPS, D), attn_gain.reshape(1, D), moe_gain.reshape(1, D), rope,
        sinks, rall, rown, router, k_cache, v_cache, w_qkv, w_out, w_gate, w_up, w_down,
    )
    return out.reshape(STEPS, 1, D)


def solution(mesh):
    nr, ns = mesh.shape["req"], mesh.shape["seq"]
    in_specs = (
        P(None, ("req", "seq"), None),
        P("req"),
        P("req", "seq", None),
        P("req", "seq", None),
        P(),
        P(),
        P(),
        P(),
        P(),
        P(),
        P(None, ("req", "seq")),
        P(None, ("req", "seq")),
        P(("req", "seq"), None),
        P(),
    )
    out_specs = P(None, ("req", "seq"), None)
    return jax.shard_map(
        functools.partial(on_device, nr, ns),
        mesh=mesh,
        in_specs=in_specs,
        out_specs=out_specs,
        check_vma=False,
    )
```

```python
import functools

import jax
import jax.numpy as jnp
from jax import lax
from jax.experimental import pallas as pl
from jax.experimental.pallas import tpu as pltpu
from jax.sharding import PartitionSpec as P

D = 1536
QH = 12
KVH = 2
HD = 128
E = 32
EFF = 768
TOP = 4
STEPS = 4
MOST = 2

ROWS = QH * STEPS
HALF = ROWS // KVH
MSG = ROWS + 16
UG = 4
UL = D // UG
OG = 6
OL = D // OG
BLK = 32
MESH = pl.DeviceIdType.MESH
F32 = jnp.float32
BF16 = jnp.bfloat16


def iota(shape, axis):
    return lax.broadcasted_iota(jnp.int32, shape, axis)


def normed(xf, gain):
    inv = lax.rsqrt(jnp.mean(xf * xf, axis=-1, keepdims=True) + 1e-05)
    return xf * inv * gain


def split3(v):
    hi = v.astype(BF16).astype(F32)
    mid = (v - hi).astype(BF16).astype(F32)
    return hi, mid, v - hi - mid


def kernel(
    nr, ns, blk, lens, sinks, x_ref, again_ref, mgain_ref, rope_ref, rall_ref, router_ref,
    kc_hbm, vc_hbm, wqkv_hbm, wout_hbm, wg_hbm, wu_hbm, wd_hbm,
    out_ref,
    wqkv, wout, wg, wu, wd, kc, vc,
    qf, kf, vf, q_all, part, part_in, uf, rows_all, prod_out, prod_in, coef,
    wsem, q_s, q_r, p_s, p_r, u_s, u_r, f_s, o_s, o_r,
):
    devs = nr * ns
    req = lax.axis_index("req")
    seq = lax.axis_index("seq")
    me = req * ns + seq
    lpos = kc.shape[1]
    window = lpos * ns
    cols = wg.shape[1]
    scale = HD ** (-0.5)
    per = EFF // cols
    shift = per.bit_length() - 1

    qparts = 4
    qrows = D // qparts
    loads = [
        pltpu.make_async_copy(
            wqkv_hbm.at[pl.ds(i * qrows, qrows)], wqkv.at[pl.ds(i * qrows, qrows)], wsem.at[i]
        )
        for i in range(qparts)
    ]
    rest = [
        pltpu.make_async_copy(src, dst, wsem.at[qparts + i])
        for i, (src, dst) in enumerate(
            [(kc_hbm, kc), (vc_hbm, vc), (wout_hbm, wout), (wg_hbm, wg), (wu_hbm, wu), (wd_hbm, wd)]
        )
    ]
    for c in loads + rest:
        c.start()
    load_k, load_v, load_out, load_g, load_u, load_d = rest

    barrier = pltpu.get_barrier_semaphore()

    def greet(i, carry):
        d = lax.rem(me + i, devs)
        pl.semaphore_signal(
            barrier, inc=1, device_id=(d // ns, lax.rem(d, ns)), device_id_type=MESH
        )
        return carry

    lax.fori_loop(1, devs, greet, 0)

    xf = x_ref[...].astype(F32)
    a = normed(xf, again_ref[...].astype(F32).reshape(1, D)).astype(BF16)
    proj = jnp.zeros((STEPS, wqkv.shape[1]), F32)
    for i in range(qparts):
        loads[i].wait()
        proj = proj + jnp.dot(
            a[:, i * qrows : (i + 1) * qrows],
            wqkv[i * qrows : (i + 1) * qrows, :],
            preferred_element_type=F32,
        )
    rope = rope_ref[seq]
    cosine = rope[0:STEPS]
    sine = rope[STEPS : 2 * STEPS]

    def rotated(head):
        v = proj[:, head * HD : (head + 1) * HD]
        return v * cosine + pltpu.roll(v, HD // 2, 1) * sine

    for head in range(QH):
        qf[head * STEPS : (head + 1) * STEPS, :] = rotated(head)
    kf[...] = jnp.zeros_like(kf)
    vf[...] = jnp.zeros_like(vf)
    for head in range(KVH):
        kf[head * STEPS : (head + 1) * STEPS, :] = rotated(QH + head)
        vf[head * STEPS : (head + 1) * STEPS, :] = proj[
            :, (QH + KVH + head) * HD : (QH + KVH + head + 1) * HD
        ]
    own_q = qf[...].astype(BF16)
    q_all[seq] = own_q

    pl.semaphore_wait(barrier, devs - 1)

    def q_copy(peer, slot, k):
        return pltpu.make_async_remote_copy(
            src_ref=q_all.at[seq], dst_ref=q_all.at[slot], send_sem=q_s.at[k],
            recv_sem=q_r.at[slot], device_id=(req, peer), device_id_type=MESH,
        )

    def q_send(i, carry):
        peer = lax.rem(seq + i, ns)
        q_copy(peer, seq, peer).start()
        return carry

    lax.fori_loop(1, ns, q_send, 0)

    row = iota((ROWS, HD), 0)
    lane = iota((ROWS, HD), 1)
    eye = row == lane

    def to_row(col):
        return jnp.sum(jnp.where(eye, col, 0.0), axis=0, keepdims=True)

    def to_col(r):
        return jnp.sum(jnp.where(eye, r, 0.0), axis=1, keepdims=True)

    tail = (
        lax.dot_general(
            own_q, kf[...].astype(BF16), (((1,), (1,)), ((), ())), preferred_element_type=F32
        )
        * scale
    )
    upper = (row >= HALF).astype(jnp.int32)
    sink_rows = jnp.zeros((ROWS, HD), F32)
    for head in range(QH):
        sink_rows = jnp.where((row >> 2) == head, sinks[head], sink_rows)
    fresh = ((lane >> 2) == upper) & ((lane & 3) <= (row & 3))
    tail = jnp.where(fresh, tail, jnp.where(lane == KVH * STEPS, sink_rows, -1e30))
    tail_peak = jnp.max(tail, axis=1, keepdims=True)
    tail_w = jnp.exp(tail - tail_peak)
    tail_total = jnp.sum(tail_w, axis=1, keepdims=True)
    tail_mixed = jnp.dot(
        tail_w.astype(BF16), vf[...].astype(BF16), preferred_element_type=F32
    )

    load_k.wait()
    load_v.wait()

    first = jnp.where(row < HALF, 1.0, 0.0).astype(BF16)
    second = jnp.where(row < HALF, 0.0, 1.0).astype(BF16)
    slot_id = seq * lpos + iota((ROWS, lpos), 1)
    step_id = iota((ROWS, lpos), 0) & 3
    stat_row = iota((16, HD), 0)

    def q_wait(i, carry):
        peer = lax.rem(seq + i, ns)
        q_copy(peer, peer, peer).wait_recv()
        return carry

    lax.fori_loop(1, ns, q_wait, 0)

    def p_copy(peer, slot, k):
        return pltpu.make_async_remote_copy(
            src_ref=part.at[peer], dst_ref=part_in.at[slot], send_sem=p_s.at[k],
            recv_sem=p_r.at[slot], device_id=(req, peer), device_id_type=MESH,
        )

    def attend(n):
        q = q_all[n]
        wide = jnp.concatenate([q * first, q * second], axis=1)
        s = (
            lax.dot_general(wide, kc[n], (((1,), (1,)), ((), ())), preferred_element_type=F32)
            * scale
        )
        length = lens[n]
        back = (length - 1 - slot_id) & (window - 1)
        valid = back < jnp.minimum(length, window - 1 - step_id)
        peak = jnp.max(jnp.where(valid, s, -1e30), axis=1, keepdims=True)
        w = jnp.where(valid, jnp.exp(s - peak), 0.0)
        total = jnp.sum(w, axis=1, keepdims=True)
        both = jnp.dot(w.astype(BF16), vc[n], preferred_element_type=F32)
        mixed = jnp.where(row < HALF, both[:, :HD], both[:, HD:])
        stats = jnp.zeros((16, HD), F32)
        for k, v in enumerate(split3(to_row(peak)) + split3(to_row(total))):
            stats = jnp.where(stat_row == k, v, stats)
        return mixed.astype(BF16), stats.astype(BF16)

    group = 4

    def attend_some(b, carry):
        for j in range(group):
            n = lax.rem(seq + 1 + b * group + j, ns)
            mixed, stats = attend(n)
            part[n, 0:ROWS, :] = mixed
            part[n, ROWS:MSG, :] = stats
        for j in range(group):
            i = b * group + j
            n = lax.rem(seq + 1 + i, ns)

            @pl.when(i < ns - 1)
            def _():
                p_copy(n, seq, n).start()

        return carry

    lax.fori_loop(0, ns // group, attend_some, 0)
    part_in[seq] = part[seq]

    def p_wait(i, carry):
        peer = lax.rem(seq + i, ns)
        p_copy(peer, peer, peer).wait_recv()
        return carry

    lax.fori_loop(1, ns, p_wait, 0)

    peaks, totals = [], []
    for j in range(ns):
        st = part_in[j, ROWS:MSG, :].astype(F32)
        peaks.append(st[0:1] + st[1:2] + st[2:3])
        totals.append(st[3:4] + st[4:5] + st[5:6])
    top = to_row(tail_peak)
    for p in peaks:
        top = jnp.maximum(top, p)
    total_row = jnp.zeros((1, HD), F32)
    mixed = jnp.zeros((ROWS, HD), F32)
    for j in range(ns):
        share = jnp.exp(peaks[j] - top)
        total_row = total_row + share * totals[j]
        mixed = mixed + to_col(share) * part_in[j, 0:ROWS, :].astype(F32)
    tail_share = jnp.exp(tail_peak - to_col(top))
    denom = to_col(total_row) + tail_total * tail_share
    qf[...] = (mixed + tail_mixed * tail_share) / denom
    attn = jnp.concatenate(
        [qf[head * STEPS : (head + 1) * STEPS, :] for head in range(QH)], axis=1
    ).astype(BF16)
    load_out.wait()
    h = (xf + jnp.dot(attn, wout[...], preferred_element_type=F32)).astype(BF16).astype(F32)
    u = normed(h, mgain_ref[...].astype(F32).reshape(1, D)).astype(BF16)
    u32 = u.astype(F32)
    for g in range(UG):
        uf[g * STEPS : (g + 1) * STEPS, :] = u32[:, g * UL : (g + 1) * UL]
    rows_all[me] = uf[...].astype(BF16)

    def u_copy(slot, k, peer):
        return pltpu.make_async_remote_copy(
            src_ref=rows_all.at[slot], dst_ref=rows_all.at[slot], send_sem=u_s.at[k],
            recv_sem=u_r.at[slot], device_id=(req, peer), device_id_type=MESH,
        )

    def f_copy(slot, k):
        return pltpu.make_async_remote_copy(
            src_ref=rows_all.at[slot], dst_ref=rows_all.at[slot], send_sem=f_s.at[k],
            recv_sem=u_r.at[slot], device_id=(1 - req, seq), device_id_type=MESH,
        )

    def u_send(i, carry):
        peer = lax.rem(seq + i, ns)
        u_copy(me, peer, peer).start()
        return carry

    lax.fori_loop(1, ns, u_send, 0)
    f_copy(me, seq).start()

    every = (STEPS, devs * 16)
    own_lane = iota(every, 1) == me * 16 + iota(every, 0)
    rown = [
        jnp.sum(
            jnp.where(own_lane, rall_ref[k : k + 1, :].astype(F32), 0.0), axis=1, keepdims=True
        )
        for k in range(TOP)
    ]
    logits = lax.dot_general(
        u, router_ref[...], (((1,), (1,)), ((), ())), preferred_element_type=F32
    )
    expert = iota((STEPS, E), 1).astype(F32)
    chosen = [
        jnp.sum(jnp.where(rown[k] == expert, logits, 0.0), axis=1, keepdims=True)
        for k in range(TOP)
    ]
    peak = functools.reduce(jnp.maximum, chosen)
    raised = [jnp.exp(c - peak) for c in chosen]
    norm = functools.reduce(jnp.add, raised)
    shares = [r / norm for r in raised]

    width = blk * 16
    nblk = devs // blk
    lane4 = iota((STEPS, width), 1)
    step4 = iota((STEPS, width), 0)
    coefs = []
    for b in range(nblk):
        source = (((lane4 >> 4) + b * blk) >> shift).astype(F32)
        hit = jnp.zeros((STEPS, width), F32)
        dense = jnp.zeros((STEPS, width), F32)
        for k in range(TOP):
            same = rown[k] == source
            hit = jnp.where(same, 1.0, hit)
            dense = jnp.where(same, shares[k], dense)
        slot = jnp.zeros((STEPS, width), F32)
        for t in range(STEPS - 1):
            slot = slot + jnp.where(step4 > t, hit[t : t + 1], 0.0)
        mine = (hit > 0.0) & (slot == (lane4 & 1).astype(F32))
        dense = jnp.where(mine, dense, 0.0)
        for k, v in enumerate(split3(dense)):
            for g in range(OG):
                at = (k * OG + g) * STEPS
                coef[b, at : at + STEPS, :] = jnp.where(((lane4 & 15) >> 1) == g, v, 0.0)

    expert_mine = (me * cols) // EFF
    pick_rows = UG * blk * MOST
    prow = iota((pick_rows, width), 0)
    plane = iota((pick_rows, width), 1)
    piece = prow // (blk * MOST)
    source_row = prow & (blk * MOST - 1)
    place_ok = ((plane >> 4) == (source_row >> 1)) & (((plane & 15) >> 2) == piece)
    want = (source_row & 1).astype(F32)
    lane8 = iota((8, width), 1)
    picks = []
    for b in range(nblk):
        hit = jnp.zeros((8, width), F32)
        for k in range(TOP):
            named = jnp.broadcast_to(rall_ref[k : k + 1, b * width : (b + 1) * width], (8, width))
            hit = jnp.where(named == expert_mine, 1.0, hit)
        slot = jnp.zeros((8, width), F32)
        for t in range(1, STEPS):
            slot = slot + jnp.where((lane8 & 3) >= t, pltpu.roll(hit, t, 1), 0.0)
        code = jnp.where(hit > 0.0, slot, -1.0)[0:1]
        picks.append(jnp.where(place_ok & (code == want), 1.0, 0.0).astype(BF16))

    out_rows = iota((width, OG * blk * MOST), 0)
    out_lane = iota((width, OG * blk * MOST), 1)
    out_piece = out_lane // (blk * MOST)
    out_source = out_lane & (blk * MOST - 1)
    spread = jnp.where(
        ((out_rows >> 4) == (out_source >> 1))
        & ((out_rows & 15) == out_piece * MOST + (out_source & 1)),
        1.0,
        0.0,
    ).astype(BF16)

    def u_wait(i, carry):
        peer = lax.rem(seq + i, ns)
        u_copy(req * ns + peer, peer, peer).wait_recv()
        f_copy(req * ns + peer, peer).start()
        return carry

    lax.fori_loop(1, ns, u_wait, 0)

    def f_wait(i, carry):
        peer = lax.rem(seq + i, ns)
        f_copy((1 - req) * ns + peer, peer).wait_recv()
        return carry

    lax.fori_loop(0, ns, f_wait, 0)

    taken = []
    for b in range(nblk):
        got = jnp.dot(
            picks[b],
            rows_all[b * blk : (b + 1) * blk].reshape(width, UL),
            preferred_element_type=F32,
        ).astype(BF16)
        taken.append(
            jnp.concatenate(
                [got[g * blk * MOST : (g + 1) * blk * MOST] for g in range(UG)], axis=1
            )
        )
    taken = jnp.concatenate(taken, axis=0) if nblk > 1 else taken[0]
    load_g.wait()
    load_u.wait()
    load_d.wait()
    gate = jnp.dot(taken, wg[...], preferred_element_type=F32)
    hidden = jnp.maximum(gate, 0.0) * jnp.dot(taken, wu[...], preferred_element_type=F32)
    made = jnp.dot(hidden.astype(BF16), wd[...], preferred_element_type=F32).astype(BF16)
    for b in range(nblk):
        stacked = jnp.concatenate(
            [
                made[b * blk * MOST : (b + 1) * blk * MOST, g * OL : (g + 1) * OL]
                for g in range(OG)
            ],
            axis=0,
        )
        prod_out[b * blk : (b + 1) * blk] = (
            jnp.dot(spread, stacked, preferred_element_type=F32).astype(BF16).reshape(blk, 16, OL)
        )

    def o_copy(d, slot, k):
        return pltpu.make_async_remote_copy(
            src_ref=prod_out.at[d], dst_ref=prod_in.at[slot], send_sem=o_s.at[k],
            recv_sem=o_r.at[slot], device_id=(d // ns, lax.rem(d, ns)), device_id_type=MESH,
        )

    def o_send(i, carry):
        d = lax.rem(me + i, devs)
        o_copy(d, me, d).start()
        return carry

    lax.fori_loop(1, devs, o_send, 0)
    prod_in[me] = prod_out[me]

    def o_wait(i, carry):
        d = lax.rem(me + i, devs)
        o_copy(d, d, d).wait_recv()
        return carry

    lax.fori_loop(1, devs, o_wait, 0)

    moe = jnp.zeros((3 * OG * STEPS, OL), F32)
    for b in range(nblk):
        moe = moe + jnp.dot(
            coef[b].astype(BF16),
            prod_in[b * blk : (b + 1) * blk].reshape(width, OL),
            preferred_element_type=F32,
        )
    span = OG * STEPS
    moe = moe[0:span] + moe[span : 2 * span] + moe[2 * span : 3 * span]
    moe = jnp.concatenate([moe[g * STEPS : (g + 1) * STEPS] for g in range(OG)], axis=1)
    out_ref[...] = (h + moe).astype(BF16)

    def drain(i, carry):
        peer = lax.rem(seq + i, ns)
        q_copy(peer, seq, peer).wait_send()
        p_copy(peer, seq, peer).wait_send()
        u_copy(me, peer, peer).wait_send()
        f_copy(req * ns + peer, peer).wait_send()
        return carry

    lax.fori_loop(1, ns, drain, 0)
    f_copy(me, seq).wait_send()

    def o_drain(i, carry):
        d = lax.rem(me + i, devs)
        o_copy(d, me, d).wait_send()
        return carry

    lax.fori_loop(1, devs, o_drain, 0)


def on_device(
    nr, ns, tokens, lengths, k_cache, v_cache, attn_gain, w_qkv, sink, w_out, moe_gain, router,
    w_gate, w_up, w_down, routes,
):
    devs = nr * ns
    blk = min(BLK, devs)
    lpos = k_cache.shape[1]
    group = lengths.shape[0]
    half = HD // 2
    shape = (group, 2 * STEPS, HD)
    row, lane = iota(shape, 1), iota(shape, 2)
    index = (lane & (half - 1)).astype(F32)
    inverse = jnp.exp(-jnp.log(1000000.0) * 2.0 * index / HD)
    angle = (lengths[:, None, None] + (row & (STEPS - 1))).astype(F32) * inverse
    sine = jnp.sin(angle)
    rope = jnp.where(row < STEPS, jnp.cos(angle), jnp.where(lane < half, -sine, sine))
    rall = jnp.broadcast_to(
        routes.transpose(2, 0, 1)[:, :, None, :], (TOP, devs, 4, STEPS)
    ).reshape(TOP, devs * 16)

    vmem = pl.BlockSpec(memory_space=pltpu.VMEM)
    smem = pl.BlockSpec(memory_space=pltpu.SMEM)
    hbm = pl.BlockSpec(memory_space=pl.ANY)
    dma = pltpu.SemaphoreType.DMA
    out = pl.pallas_call(
        functools.partial(kernel, nr, ns, blk),
        out_shape=jax.ShapeDtypeStruct((STEPS, D), BF16),
        in_specs=[smem] * 2 + [vmem] * 6 + [hbm] * 7,
        out_specs=vmem,
        scratch_shapes=[
            pltpu.VMEM(w_qkv.shape, BF16),
            pltpu.VMEM(w_out.shape, BF16),
            pltpu.VMEM(w_gate.shape, BF16),
            pltpu.VMEM(w_up.shape, BF16),
            pltpu.VMEM(w_down.shape, BF16),
            pltpu.VMEM((group, lpos, KVH * HD), BF16),
            pltpu.VMEM((group, lpos, KVH * HD), BF16),
            pltpu.VMEM((ROWS, HD), F32),
            pltpu.VMEM((HD, HD), F32),
            pltpu.VMEM((HD, HD), F32),
            pltpu.VMEM((ns, ROWS, HD), BF16),
            pltpu.VMEM((ns, MSG, HD), BF16),
            pltpu.VMEM((ns, MSG, HD), BF16),
            pltpu.VMEM((UG * STEPS, UL), F32),
            pltpu.VMEM((devs, UG * STEPS, UL), BF16),
            pltpu.VMEM((devs, 16, OL), BF16),
            pltpu.VMEM((devs, 16, OL), BF16),
            pltpu.VMEM((devs // blk, 3 * OG * STEPS, blk * 16), F32),
            dma((10,)), dma((ns,)), dma((ns,)), dma((ns,)), dma((ns,)), dma((ns,)),
            dma((devs,)), dma((ns,)), dma((devs,)), dma((devs,)),
        ],
        compiler_params=pltpu.CompilerParams(
            collective_id=0, has_side_effects=True, vmem_limit_bytes=56 * 1024 * 1024
        ),
    )(
        lengths, sink, tokens.reshape(STEPS, D), attn_gain, moe_gain, rope, rall, router.T, k_cache, v_cache, w_qkv, w_out, w_gate, w_up, w_down,
    )
    return out.reshape(STEPS, 1, D)


def solution(mesh):
    nr, ns = mesh.shape["req"], mesh.shape["seq"]
    in_specs = (
        P(None, ("req", "seq"), None),
        P("req"),
        P("req", "seq", None),
        P("req", "seq", None),
        P(),
        P(),
        P(),
        P(),
        P(),
        P(),
        P(None, ("req", "seq")),
        P(None, ("req", "seq")),
        P(("req", "seq"), None),
        P(),
    )
    out_specs = P(None, ("req", "seq"), None)
    return jax.shard_map(
        functools.partial(on_device, nr, ns),
        mesh=mesh,
        in_specs=in_specs,
        out_specs=out_specs,
        check_vma=False,
    )
```
